256 devices in a mesh: blk: 32 (over y_lo, z, core), head: 8 (over y_hi, x).
Axes of the slice: x: 4, y: 4 (y_hi: 2, y_lo: 2; y = y_hi * 2 + y_lo), z: 8, core: 2. Of those that a mesh axis runs over, the one named last changes fastest.
Arguments:
- queries: bfloat16 [32768, 2048], P(('blk', 'head')), may hold values from -4.5 to 4.5
- keys: bfloat16 [32768, 2048], P(('blk', 'head')), may hold values from -4.5 to 4.5
- values: bfloat16 [32768, 2048], P(('blk', 'head')), may hold values from -6 to 6
- grad_out: bfloat16 [32768, 2048], P(('blk', 'head')), may hold values from -6 to 6
- key_blocks: int32 [256, 16], P('blk'), may hold values from 0 to 255, as said below
- doc_lengths: int32 [8], replicated, may hold values from 1 to 8192, 32768 in all
Outputs:
- attended: bfloat16 [32768, 2048], P(('blk', 'head'))
- grad_queries: bfloat16 [32768, 2048], P(('blk', 'head'))
- grad_keys: bfloat16 [32768, 2048], P(('blk', 'head'))
- grad_values: bfloat16 [32768, 2048], P(('blk', 'head'))
The draws below stay inside these ranges and needn't reach their ends.
Inputs may be any that keep to these rules, and one draw needn't show every extreme that they name: `key_blocks`: row b lists the key blocks of query block b: its first entry is b itself, every entry lies between b - 23 and b. `doc_lengths`: the lengths sum to 32768.
All inputs are finite; a program needn't handle non-finite values.
Results may differ from the reference program's by a relative error of at most 0.011.
Values may be sent and summed in bfloat16 or wider, within the bound.
No kernel may reach another device: no remote copies, remote signals or barrier semaphores. Data moves between devices by JAX's collectives and lax.ppermute only.
A program may use at most 128 MiB of HBM per device.

```python
import math
import jax
import jax.numpy as jnp
import numpy as np
from jax import lax

H = 16
HD = 128
BLOCK = 128
KB = 16
WIN = 24
DOCS = 8
TOKENS = 32768


def draw_queries(key, part):
    key = jax.random.fold_in(key, 11)
    return jnp.clip(jax.random.normal(key, (TOKENS, H * HD), jnp.float32), -4.5, 4.5).astype(jnp.bfloat16)


def draw_keys(key, part):
    key = jax.random.fold_in(key, 12)
    return jnp.clip(jax.random.normal(key, (TOKENS, H * HD), jnp.float32), -4.5, 4.5).astype(jnp.bfloat16)


def draw_key_blocks(key, part):
    key = jax.random.fold_in(key, 13)
    block_count = TOKENS // BLOCK
    row_keys = jax.random.split(key, block_count)

    def one_row(row_key, block_id):
        distance = 1 + jax.random.permutation(row_key, WIN - 1)[:KB - 1]
        listed = block_id - distance.astype(jnp.int32)
        listed = jnp.where(listed < 0, block_id, listed)
        return jnp.concatenate([block_id[None], listed]).astype(jnp.int32)
    return jax.vmap(one_row)(row_keys, jnp.arange(block_count, dtype=jnp.int32))


def levels(stream_key, extent, shards, low, high):
    loudness, own = 1.0, jax.random.fold_in(stream_key, 6)
    for axis_at, blocks in shards:
        heights = jnp.exp(jax.random.uniform(jax.random.fold_in(own, axis_at), (blocks,), jnp.float32, low / len(shards), high / len(shards)))
        loudness = loudness * jnp.repeat(heights, extent[axis_at] // blocks).reshape([-1 if axis == axis_at else 1 for axis in range(len(extent))])
    return loudness


def split_up(count, total, reach, lean):
    weights = [(1 << 20) // math.isqrt(rank ** lean) + 1 for rank in range(2, count + 1)]
    rest, counts = total - reach - (count - 1), [1] * (count - 1)
    while rest > 0:
        free = [i for i in range(count - 1) if counts[i] < reach]
        mass, budget = sum([weights[i] for i in free]), rest
        for i in free:
            extra = min(reach - counts[i], max(1, budget * weights[i] // mass), rest)
            counts[i] = counts[i] + extra
            rest = rest - extra
    return np.array([reach] + counts)


def ragged(own_key, amount, total, reach, slope):
    if amount == 2:
        one = jax.random.randint(own_key, (), max(1, total - reach), min(reach, total - 1) + 1)
        return jnp.stack([one, total - one])
    sizes = jnp.asarray(split_up(amount, total, reach, slope), jnp.int32)
    twos = (amount - 1) // 2
    source_of, sink = sizes[1:1 + 2 * twos:2], sizes[2:2 + 2 * twos:2]
    margin = jnp.minimum(source_of - 1, reach - sink)
    passed = jax.random.randint(jax.random.fold_in(own_key, 1), (twos,), 0, 1 << 20) % (margin + 1)
    sizes = sizes.at[1:1 + 2 * twos:2].set(source_of - passed).at[2:2 + 2 * twos:2].set(sink + passed)
    return sizes[jax.random.permutation(jax.random.fold_in(own_key, 2), amount)]


def gaussian(key, extent, scale, limit, shards=(), kind=jnp.bfloat16):
    entries = scale * jax.random.normal(key, extent, jnp.float32)
    if shards:
        entries = entries * levels(key, extent, shards, -0.22, 0.18)
    return jnp.clip(entries, -limit, limit).astype(kind)


def setup_inputs(seed: int = 0) -> dict:
    seeds = jax.random.split(jax.random.key(seed), 7)
    return {
        "queries": draw_queries(jax.random.fold_in(seeds[6], 71), 0),
        "keys": draw_keys(jax.random.fold_in(seeds[6], 71), 0),
        "values": gaussian(seeds[2], (TOKENS, H * HD), 1.0, 6.0, ((0, 256),)),
        "grad_out": gaussian(seeds[3], (TOKENS, H * HD), 1.0, 6.0, ((0, 256),)),
        "key_blocks": draw_key_blocks(jax.random.fold_in(seeds[6], 71), 0),
        "doc_lengths": ragged(seeds[5], DOCS, TOKENS, TOKENS // 4, 1).astype(jnp.int32),
    }


def document_begin(positions, doc_lengths):
    lengths = doc_lengths.astype(jnp.int32)
    doc_starts = (jnp.cumsum(lengths) - lengths).astype(jnp.int32)
    earlier = doc_starts[None, :] <= positions[:, None]
    return jnp.max(jnp.where(earlier, doc_starts[None, :], 0), axis=1).astype(jnp.int32)


def tile_mask(first_query, listed, doc_lengths, block_width):
    offsets = jnp.arange(block_width, dtype=jnp.int32)
    query_pos = first_query + offsets
    key_pos = (listed[:, None] * block_width + offsets[None, :]).reshape(-1)
    ordering = jnp.arange(listed.shape[0], dtype=jnp.int32)
    repeated = jnp.any((listed[:, None] == listed[None, :]) & (ordering[:, None] > ordering[None, :]), axis=1)
    unseen = jnp.repeat(jnp.logical_not(repeated), block_width)
    starting = document_begin(query_pos, doc_lengths)
    return (key_pos[None, :] <= query_pos[:, None]) & (key_pos[None, :] >= starting[:, None]) & unseen[None, :]


def probabilities(scores, allowed):
    masked = jnp.where(allowed[None], scores, -1.0e30)
    row_peak = jnp.max(masked, axis=-1, keepdims=True)
    weights = jnp.where(allowed[None], jnp.exp(masked - row_peak), 0.0)
    return weights / jnp.sum(weights, axis=-1, keepdims=True)


def reference(queries, keys, values, grad_out, key_blocks, doc_lengths):
    block_count = queries.shape[0] // BLOCK
    head_count = queries.shape[1] // HD
    score_scale = HD ** -0.5
    shape_grid = (block_count, BLOCK, head_count, HD)
    query_grid = queries.reshape(shape_grid)
    key_grid = keys.reshape(shape_grid)
    value_grid = values.reshape(shape_grid)
    grad_grid = grad_out.reshape(shape_grid)
    block_ids = jnp.arange(block_count, dtype=jnp.int32)

    def gather_tiles(listed):
        key_tiles = key_grid[listed].reshape(KB * BLOCK, head_count, HD).astype(jnp.float32)
        value_tiles = value_grid[listed].reshape(KB * BLOCK, head_count, HD).astype(jnp.float32)
        return key_tiles, value_tiles

    def forward(inputs):
        block_id, listed, query_tile = inputs
        key_tiles, value_tiles = gather_tiles(listed)
        allowed = tile_mask(block_id * BLOCK, listed, doc_lengths, BLOCK)
        scores = jnp.einsum("qhd,khd->hqk", query_tile.astype(jnp.float32), key_tiles) * score_scale
        rounded = lax.optimization_barrier(probabilities(scores, allowed).astype(jnp.bfloat16)).astype(jnp.float32)
        return jnp.einsum("hqk,khd->qhd", rounded, value_tiles).astype(jnp.bfloat16)

    attended = lax.map(forward, (block_ids, key_blocks, query_grid))

    def backward(carried, inputs):
        key_sum, value_sum = carried
        block_id, listed, query_tile, gradient, output = inputs
        key_tiles, value_tiles = gather_tiles(listed)
        allowed = tile_mask(block_id * BLOCK, listed, doc_lengths, BLOCK)
        query_wide = query_tile.astype(jnp.float32)
        grad_wide = gradient.astype(jnp.float32)
        scores = jnp.einsum("qhd,khd->hqk", query_wide, key_tiles) * score_scale
        weights = probabilities(scores, allowed)
        rounded = lax.optimization_barrier(weights.astype(jnp.bfloat16)).astype(jnp.float32)
        row_delta = jnp.sum(grad_wide * output.astype(jnp.float32), axis=-1).T
        dprobs = jnp.einsum("qhd,khd->hqk", grad_wide, value_tiles)
        dscores = lax.optimization_barrier((weights * (dprobs - row_delta[:, :, None])).astype(jnp.bfloat16)).astype(jnp.float32)
        grad_query = (jnp.einsum("hqk,khd->qhd", dscores, key_tiles) * score_scale).astype(jnp.bfloat16)
        key_part = jnp.einsum("hqk,qhd->khd", dscores, query_wide) * score_scale
        value_part = jnp.einsum("hqk,qhd->khd", rounded, grad_wide)
        key_sum = key_sum.at[listed].add(key_part.reshape(KB, BLOCK, head_count, HD))
        value_sum = value_sum.at[listed].add(value_part.reshape(KB, BLOCK, head_count, HD))
        return (key_sum, value_sum), grad_query

    zero_sum = jnp.zeros(shape_grid, jnp.float32)
    sums, grad_queries = lax.scan(backward, (zero_sum, zero_sum), (block_ids, key_blocks, query_grid, grad_grid, attended))
    width_all = head_count * HD
    return (attended.reshape(-1, width_all), grad_queries.reshape(-1, width_all), sums[0].astype(jnp.bfloat16).reshape(-1, width_all), sums[1].astype(jnp.bfloat16).reshape(-1, width_all))
```

```python
import functools
import math

import jax
import jax.numpy as jnp
from jax import lax
from jax.experimental import pallas as pl
from jax.experimental.pallas import tpu as pltpu
from jax.sharding import Mesh
from jax.sharding import PartitionSpec as P

HD = 128
BLOCK = 128
KB = 16
WIN = 24
SCALE = HD**-0.5
LOG2E = math.log2(math.e)
GROUP = 4
CORES = ("core", "head")
NN = (((1,), (0,)), ((), ()))
TN = (((0,), (0,)), ((), ()))


def dot(a, b, dims):
    return lax.dot_general(a, b, dims, preferred_element_type=jnp.float32)


def fold(x, op):
    return op(x.reshape(BLOCK // 8, 8, BLOCK), axis=0)


def attend_kernel(
    unroll, tile_ref, start_ref, doc_ref, qg_ref, kv0_ref, kv1_ref, kv2_ref,
    out_ref, own_ref, prev_ref, far_ref, kv, acc, s_buf, d_buf, sems,
):
    far, per = far_ref.shape[0], qg_ref.shape[0]
    copies = [
        pltpu.make_async_copy(kv2_ref, kv.at[pl.ds(0, far)], sems.at[0]),
        pltpu.make_async_copy(kv1_ref, kv.at[pl.ds(far, per)], sems.at[1]),
        pltpu.make_async_copy(kv0_ref, kv.at[pl.ds(far + per, per)], sems.at[2]),
    ]
    for copy in copies:
        copy.start()
    acc[...] = jnp.zeros_like(acc)
    docs, total = [], jnp.int32(0)
    for d in range(doc_ref.shape[0]):
        docs.append(total)
        total = total + doc_ref[d]
    sub = lax.broadcasted_iota(jnp.int32, (BLOCK, BLOCK), 0)
    lane = lax.broadcasted_iota(jnp.int32, (BLOCK, BLOCK), 1)
    lane_row = lax.broadcasted_iota(jnp.int32, (1, BLOCK), 1)
    for copy in copies:
        copy.wait()

    def one(t, slot):
        s_ref, d_ref = s_buf.at[slot], d_buf.at[slot]
        q, g = qg_ref[t, 0], qg_ref[t, 1]
        qt, gt = q.T, g.T
        tiles = [tile_ref[t, i] for i in range(KB)]
        query_pos = start_ref[t, 0] + lane_row
        begin = jnp.zeros((1, BLOCK), jnp.int32)
        for first in docs:
            begin = jnp.where(first <= query_pos, first, begin)
        peak = jnp.full((8, BLOCK), -3e38, jnp.float32)
        for j in range(0, KB, GROUP):
            k_rows = jnp.concatenate([kv[tiles[i], 0] for i in range(j, j + GROUP)], axis=0)
            scores = dot(k_rows, qt, NN)
            for i in range(j, j + GROUP):
                s = scores[(i - j) * BLOCK : (i - j + 1) * BLOCK]
                allowed = sub >= begin - start_ref[t, i]
                if i == 0:
                    allowed = allowed & (sub <= lane)
                s = jnp.where(allowed, s, -1e30)
                s_ref[i] = s
                peak = jnp.maximum(peak, fold(s, jnp.max))
        for j in range(0, KB, GROUP):
            v_rows = jnp.concatenate([kv[tiles[i], 1] for i in range(j, j + GROUP)], axis=0)
            d_ref[pl.ds(j, GROUP)] = dot(v_rows, gt, NN).reshape(GROUP, BLOCK, BLOCK)
        c = SCALE * LOG2E
        peak = jnp.max(peak, axis=0, keepdims=True) * c
        sum_p = jnp.zeros((8, BLOCK), jnp.float32)
        sum_d = jnp.zeros((8, BLOCK), jnp.float32)
        for i in range(KB):
            p = jnp.exp2(s_ref[i] * c - peak)
            s_ref[i] = p
            sum_p = sum_p + fold(p, jnp.sum)
            sum_d = sum_d + fold(p * d_ref[i], jnp.sum)
        inv = 1.0 / jnp.sum(sum_p, axis=0, keepdims=True)
        delta = jnp.sum(sum_d, axis=0, keepdims=True) * inv
        attended = jnp.zeros((BLOCK, HD), jnp.float32)
        grad_q = jnp.zeros((BLOCK, HD), jnp.float32)
        for j in range(0, KB, GROUP):
            group = range(j, j + GROUP)
            p = [s_ref[i] * inv for i in group]
            p_low = jnp.concatenate([x.astype(jnp.bfloat16) for x in p], axis=0)
            ds = jnp.concatenate(
                [(p[i - j] * (d_ref[i] - delta)).astype(jnp.bfloat16) for i in group], axis=0
            )
            dv = dot(p_low, g, NN)
            for i in group:
                acc[tiles[i], 1] += dv[(i - j) * BLOCK : (i - j + 1) * BLOCK]
            dk = dot(ds, q, NN)
            for i in group:
                acc[tiles[i], 0] += dk[(i - j) * BLOCK : (i - j + 1) * BLOCK]
            attended += dot(p_low, jnp.concatenate([kv[tiles[i], 1] for i in group], axis=0), TN)
            grad_q += dot(ds, jnp.concatenate([kv[tiles[i], 0] for i in group], axis=0), TN)
        out_ref[t, 0] = attended.astype(jnp.bfloat16)
        out_ref[t, 1] = (grad_q * SCALE).astype(jnp.bfloat16)

    def step(t, _):
        for u in range(unroll):
            one(t * unroll + u, u)
        return 0

    lax.fori_loop(0, per // unroll, step, 0)
    far_ref[:, 0] = (acc[:far, 0] * SCALE).astype(jnp.bfloat16)
    far_ref[:, 1] = acc[:far, 1].astype(jnp.bfloat16)
    prev_ref[:, 0] = (acc[far : far + per, 0] * SCALE).astype(jnp.bfloat16)
    prev_ref[:, 1] = acc[far : far + per, 1].astype(jnp.bfloat16)
    own_ref[:, 0] = acc[far + per :, 0] * SCALE
    own_ref[:, 1] = acc[far + per :, 1]


def attend(tiles, starts, docs, qg, kv0, kv1, kv2, unroll):
    per, far = qg.shape[0], kv2.shape[0]
    smem = pl.BlockSpec(memory_space=pltpu.SMEM)
    vmem = pl.BlockSpec(memory_space=pltpu.VMEM)
    anywhere = pl.BlockSpec(memory_space=pl.ANY)

    def blocks(count, kind):
        return jax.ShapeDtypeStruct((count, 2, BLOCK, HD), kind)

    return pl.pallas_call(
        functools.partial(attend_kernel, unroll),
        out_shape=(
            blocks(per, jnp.bfloat16),
            blocks(per, jnp.float32),
            blocks(per, jnp.bfloat16),
            blocks(far, jnp.bfloat16),
        ),
        in_specs=[smem, smem, smem, vmem, anywhere, anywhere, anywhere],
        out_specs=(vmem,) * 4,
        scratch_shapes=[
            pltpu.VMEM((far + 2 * per, 2, BLOCK, HD), jnp.bfloat16),
            pltpu.VMEM((far + 2 * per, 2, BLOCK, HD), jnp.float32),
            pltpu.VMEM((unroll, KB, BLOCK, BLOCK), jnp.float32),
            pltpu.VMEM((unroll, KB, BLOCK, BLOCK), jnp.float32),
            pltpu.SemaphoreType.DMA((3,)),
        ],
        compiler_params=pltpu.CompilerParams(vmem_limit_bytes=48 << 20),
        cost_estimate=pl.CostEstimate(
            flops=12 * BLOCK * BLOCK * HD * KB * per,
            bytes_accessed=12 << 20,
            transcendentals=KB * per * BLOCK * BLOCK,
        ),
        name="attend",
    )(tiles, starts, docs, qg, kv0, kv1, kv2)


def shift(value, steps):
    count = lax.axis_size("yz")
    first, last = max(0, -steps), min(count, count - steps)
    return lax.ppermute(value, "yz", [(source, source + steps) for source in range(first, last)])


def to_heads(a, b):
    heads = a.shape[1] // HD
    pair = jnp.stack([a.reshape(BLOCK, heads, HD), b.reshape(BLOCK, heads, HD)])
    return lax.all_to_all(pair.transpose(2, 0, 1, 3), CORES, 0, 0, tiled=True)


def to_tokens(pair):
    pair = lax.all_to_all(pair, CORES, 0, 0, tiled=True)
    rows = pair.transpose(1, 2, 0, 3).reshape(2, BLOCK, -1)
    return rows[0], rows[1]


def on_device(queries, keys, values, grad_out, key_blocks, doc_lengths):
    per = lax.axis_size("core") * lax.axis_size("head")
    far = WIN - 1 - per
    partner = lax.ppermute(key_blocks, "core", [(0, 1), (1, 0)])
    is_first = lax.axis_index("core") == 0
    listed = jnp.concatenate(
        [jnp.where(is_first, key_blocks, partner), jnp.where(is_first, partner, key_blocks)]
    )
    order = jnp.arange(KB)
    repeated = jnp.any(
        (listed[:, :, None] == listed[:, None, :]) & (order[:, None] > order[None, :]), axis=2
    )
    tiles = listed - (lax.axis_index("yz") * per - (far + per))
    starts = jnp.where(repeated, -(1 << 30), listed * BLOCK)

    kv0 = to_heads(keys, values)
    kv1 = shift(kv0, 1)
    qg = to_heads(queries, grad_out)
    kv2 = shift(kv1[per - far :], 1)
    out, own, prev, last = attend(tiles, starts, doc_lengths, qg, kv0, kv1, kv2, 2)
    last = shift(last, -1)
    near = shift(prev[: per - far], -1)
    rest = prev[per - far :].astype(jnp.float32) + last.astype(jnp.float32)
    rest = shift(rest.astype(jnp.bfloat16), -1)
    attended, grad_q = to_tokens(out)
    grads = own + jnp.concatenate([near, rest]).astype(jnp.float32)
    grad_k, grad_v = to_tokens(grads.astype(jnp.bfloat16))
    return attended, grad_q, grad_k, grad_v


def solution(mesh):
    blk, head = mesh.devices.shape
    grid = Mesh(mesh.devices.reshape(blk // 2, 2, head), ("yz", "core", "head"))
    rows = P(("yz", "core", "head"), None)
    return jax.shard_map(
        on_device,
        mesh=grid,
        in_specs=(rows, rows, rows, rows, P(("yz", "core"), None), P()),
        out_specs=(rows,) * 4,
        check_vma=False,
    )
```

```python
import functools
import math

import jax
import jax.numpy as jnp
from jax import lax
from jax.experimental import pallas as pl
from jax.experimental.pallas import tpu as pltpu
from jax.sharding import Mesh
from jax.sharding import PartitionSpec as P

HD = 128
BLOCK = 128
KB = 16
WIN = 24
SCALE = HD**-0.5
EXPONENT = SCALE * math.log2(math.e)
GROUP = 4
CORES = ("core", "head")
NN = (((1,), (0,)), ((), ()))
NT = (((1,), (1,)), ((), ()))
TN = (((0,), (0,)), ((), ()))
SMEM = pl.BlockSpec(memory_space=pltpu.SMEM)
VMEM = pl.BlockSpec(memory_space=pltpu.VMEM)
ANYWHERE = pl.BlockSpec(memory_space=pltpu.HBM)


def dot(a, b, dims):
    return lax.dot_general(a, b, dims, preferred_element_type=jnp.float32)


def fold(x, op):
    return op(x.reshape(BLOCK // 8, 8, BLOCK), axis=0)


def rows_of(ref, tiles):
    return jnp.concatenate([ref[tile] for tile in tiles], axis=0)


def part(x, i):
    return x[i * BLOCK : (i + 1) * BLOCK]


def corners(pair):
    zero = jnp.zeros((BLOCK, HD), pair.dtype)
    top = jnp.concatenate([pair[:, :HD], zero], axis=1)
    return jnp.concatenate([top, jnp.concatenate([zero, pair[:, HD:]], axis=1)], axis=0)


def start_copies(pieces, target, sems, first):
    copies, at = [], 0
    for i, (ref, begin, count) in enumerate(pieces):
        copies.append(
            pltpu.make_async_copy(
                ref.at[pl.ds(begin, count)], target.at[pl.ds(at, count)], sems.at[first + i]
            )
        )
        at += count
    for copy in copies:
        copy.start()
    return copies


def doc_starts(doc_ref):
    starts, total = [], jnp.int32(0)
    for d in range(doc_ref.shape[0]):
        starts.append(total)
        total = total + doc_ref[d]
    return starts


def doc_begin(starts, query_pos):
    begin = jnp.zeros_like(query_pos)
    for start in starts:
        begin = jnp.where(start <= query_pos, start, begin)
    return begin


def blocks(count, kind):
    return jax.ShapeDtypeStruct((count, BLOCK, 2 * HD), kind)


def cost(tiles, matmuls):
    return pl.CostEstimate(
        flops=matmuls * tiles * BLOCK * BLOCK * HD // 4,
        bytes_accessed=1 << 20,
        transcendentals=0,
    )


def total_of(pieces):
    return sum(count for _, _, count in pieces)


def queries_kernel(unroll, first, count, shift_by, spans, done,
                   tile_ref, start_ref, doc_ref, qg_ref, *refs):
    kv_refs, refs = refs[: len(spans)], refs[len(spans) :]
    out_ref, stat_ref, kv, s_buf, d_buf, sems = refs[-6:]
    pieces = [(ref, *span) for ref, span in zip(kv_refs, spans)]
    copies = start_copies(pieces, kv, sems, 0)
    if done:
        rest = pl.ds(count, done)
        finished = [
            pltpu.make_async_copy(refs[0], out_ref.at[rest], sems.at[len(spans)]),
            pltpu.make_async_copy(refs[1], stat_ref.at[rest], sems.at[len(spans) + 1]),
        ]
        for copy in finished:
            copy.start()
    starts = doc_starts(doc_ref)
    sub = lax.broadcasted_iota(jnp.int32, (BLOCK, BLOCK), 0)
    lane = lax.broadcasted_iota(jnp.int32, (BLOCK, BLOCK), 1)
    lane_row = lax.broadcasted_iota(jnp.int32, (1, BLOCK), 1)
    for copy in copies:
        copy.wait()

    def one(t, slot):
        s_ref, d_ref = s_buf.at[slot], d_buf.at[slot]
        row = first + t
        qt, gt = qg_ref[row][:, :HD].T, qg_ref[row][:, HD:].T
        tiles = [tile_ref[row, i] - shift_by for i in range(KB)]
        begin = doc_begin(starts, start_ref[row, 0] + lane_row)
        peak = jnp.full((8, BLOCK), -3e38, jnp.float32)
        for j in range(0, KB, GROUP):
            scores = dot(rows_of(kv, tiles[j : j + GROUP])[:, :HD], qt, NN)
            for i in range(j, j + GROUP):
                allowed = sub >= begin - start_ref[row, i]
                if i == 0:
                    allowed = allowed & (sub <= lane)
                s = jnp.where(allowed, part(scores, i - j), -1e30)
                s_ref[i] = s
                peak = jnp.maximum(peak, fold(s, jnp.max))
        for j in range(0, KB, GROUP):
            d_rows = dot(rows_of(kv, tiles[j : j + GROUP])[:, HD:], gt, NN)
            d_ref[pl.ds(j, GROUP)] = d_rows.reshape(GROUP, BLOCK, BLOCK)
        peak = jnp.max(peak, axis=0, keepdims=True) * EXPONENT
        sum_p = jnp.zeros((8, BLOCK), jnp.float32)
        sum_d = jnp.zeros((8, BLOCK), jnp.float32)
        for i in range(KB):
            p = jnp.exp2(s_ref[i] * EXPONENT - peak)
            s_ref[i] = p
            sum_p = sum_p + fold(p, jnp.sum)
            sum_d = sum_d + fold(p * d_ref[i], jnp.sum)
        total = jnp.sum(sum_p, axis=0, keepdims=True)
        inv = 1.0 / total
        delta = jnp.sum(sum_d, axis=0, keepdims=True) * inv
        stat_ref[t, 0:1] = peak + jnp.log2(total)
        stat_ref[t, 1:2] = delta
        attended = jnp.zeros((BLOCK, HD), jnp.float32)
        grad_q = jnp.zeros((BLOCK, HD), jnp.float32)
        for j in range(0, KB, GROUP):
            group = range(j, j + GROUP)
            p = [s_ref[i] * inv for i in group]
            p_low = jnp.concatenate([x.astype(jnp.bfloat16) for x in p], axis=0)
            ds = jnp.concatenate(
                [(p[i - j] * (d_ref[i] - delta)).astype(jnp.bfloat16) for i in group], axis=0
            )
            kv_rows = rows_of(kv, tiles[j : j + GROUP])
            attended += dot(p_low, kv_rows[:, HD:], TN)
            grad_q += dot(ds, kv_rows[:, :HD], TN)
        out_ref[t, :, :HD] = attended.astype(jnp.bfloat16)
        out_ref[t, :, HD:] = (grad_q * SCALE).astype(jnp.bfloat16)

    def step(t, _):
        for u in range(unroll):
            one(t * unroll + u, u)
        return 0

    lax.fori_loop(0, count // unroll, step, 0)
    if done:
        for copy in finished:
            copy.wait()


def attend(tiles, starts, docs, qg, first, count, shift_by, pieces, done, after, unroll=4):
    spans = [piece[1:] for piece in pieces]
    done_rows = done[0].shape[0] if done else 0
    extra = [piece[0] for piece in pieces] + list(done) + list(after)
    return pl.pallas_call(
        functools.partial(queries_kernel, unroll, first, count, shift_by, spans, done_rows),
        out_shape=(
            blocks(count + done_rows, jnp.bfloat16),
            jax.ShapeDtypeStruct((count + done_rows, 2, BLOCK), jnp.float32),
        ),
        in_specs=[SMEM, SMEM, SMEM, VMEM] + [ANYWHERE] * len(extra),
        out_specs=(VMEM, VMEM),
        scratch_shapes=[
            pltpu.VMEM((total_of(pieces), BLOCK, 2 * HD), jnp.bfloat16),
            pltpu.VMEM((unroll, KB, BLOCK, BLOCK), jnp.float32),
            pltpu.VMEM((unroll, KB, BLOCK, BLOCK), jnp.float32),
            pltpu.SemaphoreType.DMA((len(pieces) + 2,)),
        ],
        compiler_params=pltpu.CompilerParams(vmem_limit_bytes=32 << 20),
        cost_estimate=cost(count * KB, 4),
        name="attend",
    )(tiles, starts, docs, qg, *extra)


def keys_kernel(
    unroll, rows, first, gap_at, gap, spans, n_qg, n_stat, carried,
    count_ref, tile_ref, doc_ref, base_ref, kv_ref, *refs,
):
    pieces = [(ref, *span) for ref, span in zip(refs, spans)]
    out_ref, qg, stat, acc, row_of, slot_of, sems = refs[-7:]
    copies = start_copies(pieces[:n_qg], qg, sems, 0)
    copies += start_copies(pieces[n_qg : n_qg + n_stat], stat, sems, n_qg)
    copies += start_copies(pieces[n_qg + n_stat :], acc, sems, n_qg + n_stat)
    if not carried:
        acc[...] = jnp.zeros_like(acc)
    starts = doc_starts(doc_ref)
    base = base_ref[0]
    sub = lax.broadcasted_iota(jnp.int32, (BLOCK, BLOCK), 0)
    lane_row = lax.broadcasted_iota(jnp.int32, (1, BLOCK), 1)

    def listed_row(r):
        return first + r + jnp.where(r >= gap_at, gap, 0)

    def list_row(r, at):
        def put(k, at):
            row_of[at] = r
            slot_of[at] = k * GROUP
            return at + 1

        groups = (count_ref[listed_row(r)] + (GROUP - 1)) >> (GROUP.bit_length() - 1)
        return lax.fori_loop(0, groups, put, at)

    items = lax.fori_loop(0, rows, list_row, jnp.int32(0))
    for u in range(unroll):
        row_of[items + u] = 0
        slot_of[items + u] = KB
    for copy in copies:
        copy.wait()

    def one(item):
        r, slot = row_of[item], slot_of[item]
        row = listed_row(r)
        count = count_ref[row]
        both = corners(qg[r])
        query_pos = base + row * BLOCK + lane_row
        begin = doc_begin(starts, query_pos)
        peak, delta = stat[r, 0:1], stat[r, 1:2]
        tiles = [tile_ref[row, slot + i] for i in range(GROUP)]
        scores = dot(rows_of(kv_ref, tiles), both, NT)
        weights = []
        for i in range(GROUP):
            start = jnp.where(slot + i < count, base + tiles[i] * BLOCK, 1 << 30)
            allowed = (sub >= begin - start) & (sub <= query_pos - start)
            s = part(scores, i)
            p = jnp.where(allowed, jnp.exp2(s[:, :BLOCK] * EXPONENT - peak), 0.0)
            ds = (p * (s[:, BLOCK:] - delta)).astype(jnp.bfloat16)
            weights.append(jnp.concatenate([ds, p.astype(jnp.bfloat16)], axis=1))
        return tiles, dot(jnp.concatenate(weights, axis=0), both, NN)

    def step(t, _):
        results = [one(t * unroll + u) for u in range(unroll)]
        for tiles, grads in results:
            for i in range(GROUP):
                acc[tiles[i]] += part(grads, i)
        return 0

    lax.fori_loop(0, lax.div(items + (unroll - 1), jnp.int32(unroll)), step, 0)
    if carried:
        out_ref[:, :, :HD] = (acc[:, :, :HD] * SCALE).astype(jnp.bfloat16)
        out_ref[:, :, HD:] = acc[:, :, HD:].astype(jnp.bfloat16)
    else:
        out_ref[...] = acc[...]


def key_grads(counts, tiles, docs, base, kv, first, gap_at, gap, qg, stat, carried, unroll=12):
    per, rows = kv.shape[0], total_of(qg)
    pieces = [*qg, *stat, *carried]
    spans = [piece[1:] for piece in pieces]
    items = rows * (KB // GROUP) + unroll
    return pl.pallas_call(
        functools.partial(
            keys_kernel, unroll, rows, first, gap_at, gap, spans, len(qg), len(stat), len(carried)
        ),
        out_shape=blocks(per, jnp.bfloat16 if carried else jnp.float32),
        in_specs=[SMEM, SMEM, SMEM, SMEM, VMEM] + [ANYWHERE] * len(pieces),
        out_specs=VMEM,
        scratch_shapes=[
            pltpu.VMEM((rows, BLOCK, 2 * HD), jnp.bfloat16),
            pltpu.VMEM((rows, 2, BLOCK), jnp.float32),
            pltpu.VMEM((per, BLOCK, 2 * HD), jnp.float32),
            pltpu.SMEM((items,), jnp.int32),
            pltpu.SMEM((items,), jnp.int32),
            pltpu.SemaphoreType.DMA((len(pieces),)),
        ],
        compiler_params=pltpu.CompilerParams(vmem_limit_bytes=32 << 20),
        cost_estimate=cost(rows * 8, 4),
        name="key_grads",
    )(counts, tiles, docs, base, kv, *[piece[0] for piece in pieces])


def run_copies(pairs, sems):
    copies = [
        pltpu.make_async_copy(source, target, sems.at[i])
        for i, (source, target) in enumerate(pairs)
    ]
    for copy in copies:
        copy.start()
    for copy in copies:
        copy.wait()


def columns(i):
    return pl.ds(i * HD, HD)


def pack_kernel(*refs):
    *ins, out_ref, sems = refs
    pairs = []
    for h in range(out_ref.shape[0]):
        for j, ref in enumerate(ins):
            pairs.append((ref.at[:, columns(h)], out_ref.at[h, j // 2, :, columns(j % 2)]))
    run_copies(pairs, sems)


def to_heads(*arrays):
    heads = arrays[0].shape[1] // HD
    packed = pl.pallas_call(
        pack_kernel,
        out_shape=jax.ShapeDtypeStruct((heads, len(arrays) // 2, BLOCK, 2 * HD), jnp.bfloat16),
        in_specs=[ANYWHERE] * len(arrays),
        out_specs=VMEM,
        scratch_shapes=[pltpu.SemaphoreType.DMA((heads * len(arrays),))],
        name="pack",
    )(*arrays)
    return lax.all_to_all(packed, CORES, 0, 0, tiled=True)


def unpack_kernel(pair_ref, a_ref, b_ref, sems):
    pairs = []
    for h in range(pair_ref.shape[0]):
        for j, ref in enumerate((a_ref, b_ref)):
            pairs.append((pair_ref.at[h, :, columns(j)], ref.at[:, columns(h)]))
    run_copies(pairs, sems)


def to_tokens(pair):
    pair = lax.all_to_all(pair, CORES, 0, 0, tiled=True)
    rows = jax.ShapeDtypeStruct((BLOCK, pair.shape[0] * HD), jnp.bfloat16)
    return pl.pallas_call(
        unpack_kernel,
        out_shape=(rows, rows),
        in_specs=[VMEM],
        out_specs=(VMEM, VMEM),
        scratch_shapes=[pltpu.SemaphoreType.DMA((2 * pair.shape[0],))],
        name="unpack",
    )(pair)


def shift(value, steps):
    count = lax.axis_size("yz")
    first, last = max(0, -steps), min(count, count - steps)
    return lax.ppermute(value, "yz", [(source, source + steps) for source in range(first, last)])


def on_device(queries, keys, values, grad_out, key_blocks, doc_lengths):
    per = lax.axis_size("core") * lax.axis_size("head")
    total = lax.axis_size("yz") * per
    far, half = WIN - 1 - per, per // 2
    first_block = lax.axis_index("yz") * per

    partner = lax.ppermute(key_blocks, "core", [(0, 1), (1, 0)])
    is_first = lax.axis_index("core") == 0
    listed = jnp.concatenate(
        [jnp.where(is_first, key_blocks, partner), jnp.where(is_first, partner, key_blocks)]
    )
    listed = jnp.concatenate([listed, shift(listed, -1), shift(listed[:far], -2)])
    everything = to_heads(keys, values, queries, grad_out)
    kv0, qg0 = everything[:, 0], everything[:, 1]
    kv1_high, qg1_low = shift(everything[per - far :, 0], 1), shift(everything[:far, 1], -1)
    kv1_low, qg1_high = shift(everything[: per - far, 0], 1), shift(everything[far:, 1], -1)
    kv2, qg2 = shift(kv1_high, 1), shift(qg1_low, -1)
    kv1 = [(kv1_low, 0, per - far), (kv1_high, 0, far)]
    qg1 = [(qg1_low, 0, far), (qg1_high, 0, per - far)]

    order = jnp.arange(KB)
    earlier = order[:, None] > order[None, :]
    repeated = jnp.any((listed[:, :, None] == listed[:, None, :]) & earlier, axis=2)
    tiles = listed[:per] - (first_block - (far + per))
    starts = jnp.where(repeated[:per], -(1 << 30), listed[:per] * BLOCK)
    local = listed - first_block
    real = first_block + jnp.arange(listed.shape[0]) < total
    wanted = (local >= 0) & (local < per) & jnp.logical_not(repeated) & real[:, None]
    rank = jnp.sum(jnp.where(wanted[:, None, :] & earlier, 1, 0), axis=2)
    taken = wanted[:, :, None] & (rank[:, :, None] == jnp.arange(KB + GROUP))
    own_tiles = jnp.sum(jnp.where(taken, local[:, :, None], 0), axis=1)
    counts = jnp.sum(wanted.astype(jnp.int32), axis=1)
    base = (first_block * BLOCK).reshape(1)

    late, late_stat = attend(
        tiles, starts, doc_lengths, qg0, half, half, far, [*kv1, (kv0, 0, per)], [], [qg1_low, qg1_high]
    )
    both, stat = attend(
        tiles, starts, doc_lengths, qg0, 0, half, 0,
        [(kv2, 0, far), *kv1, (kv0, 0, half)], [late, late_stat], [qg2],
    )
    sums = key_grads(
        counts, own_tiles, doc_lengths, base, kv0, 0, per, 0,
        [(qg0, 0, per)], [(stat, 0, per)], [],
    )
    attended, grad_q = to_tokens(both)
    grads = key_grads(
        counts, own_tiles, doc_lengths, base, kv0, per, per, 0,
        [*qg1, (qg2, 0, far)],
        [(shift(stat, -1), 0, per), (shift(stat, -2), 0, far)],
        [(sums, 0, per)],
    )
    grad_k, grad_v = to_tokens(grads)
    return attended, grad_q, grad_k, grad_v


def solution(mesh):
    blk, head = mesh.devices.shape
    grid = Mesh(mesh.devices.reshape(blk // 2, 2, head), ("yz", "core", "head"))
    rows = P(("yz", "core", "head"), None)
    return jax.shard_map(
        on_device,
        mesh=grid,
        in_specs=(rows, rows, rows, rows, P(("yz", "core"), None), P()),
        out_specs=(rows,) * 4,
        check_vma=False,
    )
```

```python
import functools
import math

import jax
import jax.numpy as jnp
from jax import lax
from jax.experimental import pallas as pl
from jax.experimental.pallas import tpu as pltpu
from jax.sharding import Mesh
from jax.sharding import PartitionSpec as P

HD = 128
BLOCK = 128
KB = 16
WIN = 24
SCALE = HD**-0.5
EXPONENT = SCALE * math.log2(math.e)
GROUP = 4
CORES = ("core", "head")
NN = (((1,), (0,)), ((), ()))
NT = (((1,), (1,)), ((), ()))
TN = (((0,), (0,)), ((), ()))
SMEM = pl.BlockSpec(memory_space=pltpu.SMEM)
VMEM = pl.BlockSpec(memory_space=pltpu.VMEM)
ANYWHERE = pl.BlockSpec(memory_space=pltpu.HBM)


def dot(a, b, dims):
    return lax.dot_general(a, b, dims, preferred_element_type=jnp.float32)


def fold(x, op):
    return op(x.reshape(BLOCK // 8, 8, BLOCK), axis=0)


def rows_of(ref, tiles):
    return jnp.concatenate([ref[tile] for tile in tiles], axis=0)


def part(x, i):
    return x[i * BLOCK : (i + 1) * BLOCK]


def corners(pair):
    zero = jnp.zeros((BLOCK, HD), pair.dtype)
    top = jnp.concatenate([pair[:, :HD], zero], axis=1)
    return jnp.concatenate([top, jnp.concatenate([zero, pair[:, HD:]], axis=1)], axis=0)


def start_copies(pieces, target, sems, first):
    copies, at = [], 0
    for i, (ref, begin, count) in enumerate(pieces):
        copies.append(
            pltpu.make_async_copy(
                ref.at[pl.ds(begin, count)], target.at[pl.ds(at, count)], sems.at[first + i]
            )
        )
        at += count
    for copy in copies:
        copy.start()
    return copies


def doc_starts(doc_ref):
    starts, total = [], jnp.int32(0)
    for d in range(doc_ref.shape[0]):
        starts.append(total)
        total = total + doc_ref[d]
    return starts


def doc_begin(starts, query_pos):
    begin = jnp.zeros_like(query_pos)
    for start in starts:
        begin = jnp.where(start <= query_pos, start, begin)
    return begin


def blocks(count, kind):
    return jax.ShapeDtypeStruct((count, BLOCK, 2 * HD), kind)


def cost(tiles, matmuls):
    return pl.CostEstimate(
        flops=matmuls * tiles * BLOCK * BLOCK * HD // 4,
        bytes_accessed=1 << 20,
        transcendentals=0,
    )


def total_of(pieces):
    return sum(count for _, _, count in pieces)


def queries_kernel(unroll, first, count, shift_by, spans, done,
                   tile_ref, start_ref, doc_ref, qg_ref, *refs):
    kv_refs, refs = refs[: len(spans)], refs[len(spans) :]
    out_ref, stat_ref, kv, s_buf, d_buf, sems = refs[-6:]
    pieces = [(ref, *span) for ref, span in zip(kv_refs, spans)]
    copies = start_copies(pieces, kv, sems, 0)
    if done:
        rest = pl.ds(count, done)
        finished = [
            pltpu.make_async_copy(refs[0], out_ref.at[rest], sems.at[len(spans)]),
            pltpu.make_async_copy(refs[1], stat_ref.at[rest], sems.at[len(spans) + 1]),
        ]
        for copy in finished:
            copy.start()
    starts = doc_starts(doc_ref)
    sub = lax.broadcasted_iota(jnp.int32, (BLOCK, BLOCK), 0)
    lane = lax.broadcasted_iota(jnp.int32, (BLOCK, BLOCK), 1)
    lane_row = lax.broadcasted_iota(jnp.int32, (1, BLOCK), 1)
    for copy in copies:
        copy.wait()

    def one(t, slot):
        s_ref, d_ref = s_buf.at[slot], d_buf.at[slot]
        row = first + t
        qt, gt = qg_ref[row][:, :HD].T, qg_ref[row][:, HD:].T
        tiles = [tile_ref[row, i] - shift_by for i in range(KB)]
        begin = doc_begin(starts, start_ref[row, 0] + lane_row)
        peak = jnp.full((8, BLOCK), -3e38, jnp.float32)
        for j in range(0, KB, GROUP):
            scores = dot(rows_of(kv, tiles[j : j + GROUP])[:, :HD], qt, NN)
            for i in range(j, j + GROUP):
                allowed = sub >= begin - start_ref[row, i]
                if i == 0:
                    allowed = allowed & (sub <= lane)
                s = jnp.where(allowed, part(scores, i - j), -1e30)
                s_ref[i] = s
                peak = jnp.maximum(peak, fold(s, jnp.max))
        for j in range(0, KB, GROUP):
            d_rows = dot(rows_of(kv, tiles[j : j + GROUP])[:, HD:], gt, NN)
            d_ref[pl.ds(j, GROUP)] = d_rows.reshape(GROUP, BLOCK, BLOCK)
        peak = jnp.max(peak, axis=0, keepdims=True) * EXPONENT
        sum_p = jnp.zeros((8, BLOCK), jnp.float32)
        sum_d = jnp.zeros((8, BLOCK), jnp.float32)
        for i in range(KB):
            p = jnp.exp2(s_ref[i] * EXPONENT - peak)
            s_ref[i] = p
            sum_p = sum_p + fold(p, jnp.sum)
            sum_d = sum_d + fold(p * d_ref[i], jnp.sum)
        total = jnp.sum(sum_p, axis=0, keepdims=True)
        inv = 1.0 / total
        delta = jnp.sum(sum_d, axis=0, keepdims=True) * inv
        stat_ref[t, 0:1] = peak + jnp.log2(total)
        stat_ref[t, 1:2] = delta
        attended = jnp.zeros((BLOCK, HD), jnp.float32)
        grad_q = jnp.zeros((BLOCK, HD), jnp.float32)
        for j in range(0, KB, GROUP):
            group = range(j, j + GROUP)
            p = [s_ref[i] * inv for i in group]
            p_low = jnp.concatenate([x.astype(jnp.bfloat16) for x in p], axis=0)
            ds = jnp.concatenate(
                [(p[i - j] * (d_ref[i] - delta)).astype(jnp.bfloat16) for i in group], axis=0
            )
            kv_rows = rows_of(kv, tiles[j : j + GROUP])
            attended += dot(p_low, kv_rows[:, HD:], TN)
            grad_q += dot(ds, kv_rows[:, :HD], TN)
        out_ref[t, :, :HD] = attended.astype(jnp.bfloat16)
        out_ref[t, :, HD:] = (grad_q * SCALE).astype(jnp.bfloat16)

    def step(t, _):
        for u in range(unroll):
            one(t * unroll + u, u)
        return 0

    lax.fori_loop(0, count // unroll, step, 0)
    if done:
        for copy in finished:
            copy.wait()


def attend(tiles, starts, docs, qg, first, count, shift_by, pieces, done, after, unroll=4):
    spans = [piece[1:] for piece in pieces]
    done_rows = done[0].shape[0] if done else 0
    extra = [piece[0] for piece in pieces] + list(done) + list(after)
    return pl.pallas_call(
        functools.partial(queries_kernel, unroll, first, count, shift_by, spans, done_rows),
        out_shape=(
            blocks(count + done_rows, jnp.bfloat16),
            jax.ShapeDtypeStruct((count + done_rows, 2, BLOCK), jnp.float32),
        ),
        in_specs=[SMEM, SMEM, SMEM, VMEM] + [ANYWHERE] * len(extra),
        out_specs=(VMEM, VMEM),
        scratch_shapes=[
            pltpu.VMEM((total_of(pieces), BLOCK, 2 * HD), jnp.bfloat16),
            pltpu.VMEM((unroll, KB, BLOCK, BLOCK), jnp.float32),
            pltpu.VMEM((unroll, KB, BLOCK, BLOCK), jnp.float32),
            pltpu.SemaphoreType.DMA((len(pieces) + 2,)),
        ],
        compiler_params=pltpu.CompilerParams(vmem_limit_bytes=32 << 20),
        cost_estimate=cost(count * KB, 4),
        name="attend",
    )(tiles, starts, docs, qg, *extra)


def keys_kernel(
    unroll, rows, spans, n_qg,
    count_ref, tile_ref, doc_ref, base_ref, kv_ref, *refs,
):
    pieces = [(ref, *span) for ref, span in zip(refs, spans)]
    out_ref, qg, stat, acc, row_of, slot_of, sems = refs[-7:]
    copies = start_copies(pieces[:n_qg], qg, sems, 0)
    copies += start_copies(pieces[n_qg:], stat, sems, n_qg)
    acc[...] = jnp.zeros_like(acc)
    starts = doc_starts(doc_ref)
    base = base_ref[0]
    sub = lax.broadcasted_iota(jnp.int32, (BLOCK, BLOCK), 0)
    lane_row = lax.broadcasted_iota(jnp.int32, (1, BLOCK), 1)

    def list_row(r, at):
        def put(k, at):
            row_of[at] = r
            slot_of[at] = k * GROUP
            return at + 1

        groups = (count_ref[r] + (GROUP - 1)) >> (GROUP.bit_length() - 1)
        return lax.fori_loop(0, groups, put, at)

    items = lax.fori_loop(0, rows, list_row, jnp.int32(0))
    for u in range(unroll):
        row_of[items + u] = 0
        slot_of[items + u] = KB
    for copy in copies:
        copy.wait()

    def one(item):
        r, slot = row_of[item], slot_of[item]
        count = count_ref[r]
        both = corners(qg[r])
        query_pos = base + r * BLOCK + lane_row
        begin = doc_begin(starts, query_pos)
        peak, delta = stat[r, 0:1], stat[r, 1:2]
        tiles = [tile_ref[r, slot + i] for i in range(GROUP)]
        scores = dot(rows_of(kv_ref, tiles), both, NT)
        weights = []
        for i in range(GROUP):
            start = jnp.where(slot + i < count, base + tiles[i] * BLOCK, 1 << 30)
            allowed = (sub >= begin - start) & (sub <= query_pos - start)
            s = part(scores, i)
            p = jnp.where(allowed, jnp.exp2(s[:, :BLOCK] * EXPONENT - peak), 0.0)
            ds = (p * (s[:, BLOCK:] - delta)).astype(jnp.bfloat16)
            weights.append(jnp.concatenate([ds, p.astype(jnp.bfloat16)], axis=1))
        return tiles, dot(jnp.concatenate(weights, axis=0), both, NN)

    def step(t, _):
        results = [one(t * unroll + u) for u in range(unroll)]
        for tiles, grads in results:
            for i in range(GROUP):
                acc[tiles[i]] += part(grads, i)
        return 0

    lax.fori_loop(0, lax.div(items + (unroll - 1), jnp.int32(unroll)), step, 0)
    out_ref[:, :, :HD] = (acc[:, :, :HD] * SCALE).astype(jnp.bfloat16)
    out_ref[:, :, HD:] = acc[:, :, HD:].astype(jnp.bfloat16)


def key_grads(counts, tiles, docs, base, kv, qg, stat, unroll=12):
    per, rows = kv.shape[0], total_of(qg)
    pieces = [*qg, *stat]
    spans = [piece[1:] for piece in pieces]
    items = rows * (KB // GROUP) + unroll
    return pl.pallas_call(
        functools.partial(keys_kernel, unroll, rows, spans, len(qg)),
        out_shape=blocks(per, jnp.bfloat16),
        in_specs=[SMEM, SMEM, SMEM, SMEM, VMEM] + [ANYWHERE] * len(pieces),
        out_specs=VMEM,
        scratch_shapes=[
            pltpu.VMEM((rows, BLOCK, 2 * HD), jnp.bfloat16),
            pltpu.VMEM((rows, 2, BLOCK), jnp.float32),
            pltpu.VMEM((per, BLOCK, 2 * HD), jnp.float32),
            pltpu.SMEM((items,), jnp.int32),
            pltpu.SMEM((items,), jnp.int32),
            pltpu.SemaphoreType.DMA((len(pieces),)),
        ],
        compiler_params=pltpu.CompilerParams(vmem_limit_bytes=32 << 20),
        cost_estimate=cost(rows * 8, 4),
        name="key_grads",
    )(counts, tiles, docs, base, kv, *[piece[0] for piece in pieces])


def run_copies(pairs, sems):
    copies = [
        pltpu.make_async_copy(source, target, sems.at[i])
        for i, (source, target) in enumerate(pairs)
    ]
    for copy in copies:
        copy.start()
    for copy in copies:
        copy.wait()


def columns(i):
    return pl.ds(i * HD, HD)


def pack_kernel(count, *refs):
    ins, (out_ref, held, in_sems, sems) = refs[:count], refs[-4:]
    arrive = [
        pltpu.make_async_copy(ref, held.at[j], in_sems.at[j]) for j, ref in enumerate(ins)
    ]
    for copy in arrive:
        copy.start()
    leave = []
    for j in range(count):
        arrive[j].wait()
        for h in range(out_ref.shape[0]):
            leave.append(
                pltpu.make_async_copy(
                    held.at[j, :, columns(h)],
                    out_ref.at[h, j // 2, :, columns(j % 2)],
                    sems.at[j, h],
                )
            )
            leave[-1].start()
    for copy in leave:
        copy.wait()


def to_heads(*arrays):
    heads = arrays[0].shape[1] // HD
    packed = pl.pallas_call(
        functools.partial(pack_kernel, len(arrays)),
        out_shape=jax.ShapeDtypeStruct((heads, len(arrays) // 2, BLOCK, 2 * HD), jnp.bfloat16),
        in_specs=[ANYWHERE] * len(arrays),
        out_specs=ANYWHERE,
        scratch_shapes=[
            pltpu.VMEM((len(arrays), *arrays[0].shape), jnp.bfloat16),
            pltpu.SemaphoreType.DMA((len(arrays),)),
            pltpu.SemaphoreType.DMA((len(arrays), heads)),
        ],
        name="pack",
    )(*arrays)
    return lax.all_to_all(packed, CORES, 0, 0, tiled=True)


def unpack_kernel(pair_ref, a_ref, b_ref, sems):
    pairs = []
    for h in range(pair_ref.shape[0]):
        for j, ref in enumerate((a_ref, b_ref)):
            pairs.append((pair_ref.at[h, :, columns(j)], ref.at[:, columns(h)]))
    run_copies(pairs, sems)


def to_tokens(pair):
    pair = lax.all_to_all(pair, CORES, 0, 0, tiled=True)
    rows = jax.ShapeDtypeStruct((BLOCK, pair.shape[0] * HD), jnp.bfloat16)
    return pl.pallas_call(
        unpack_kernel,
        out_shape=(rows, rows),
        in_specs=[VMEM],
        out_specs=(ANYWHERE, ANYWHERE),
        scratch_shapes=[pltpu.SemaphoreType.DMA((2 * pair.shape[0],))],
        name="unpack",
    )(pair)


def shift(value, steps):
    count = lax.axis_size("yz")
    first, last = max(0, -steps), min(count, count - steps)
    return lax.ppermute(value, "yz", [(source, source + steps) for source in range(first, last)])


def on_device(queries, keys, values, grad_out, key_blocks, doc_lengths):
    per = lax.axis_size("core") * lax.axis_size("head")
    total = lax.axis_size("yz") * per
    far, half = WIN - 1 - per, per // 2
    first_block = lax.axis_index("yz") * per

    partner = lax.ppermute(key_blocks, "core", [(0, 1), (1, 0)])
    is_first = lax.axis_index("core") == 0
    listed = jnp.concatenate(
        [jnp.where(is_first, key_blocks, partner), jnp.where(is_first, partner, key_blocks)]
    )
    listed = jnp.concatenate([listed, shift(listed, -1), shift(listed[:far], -2)])
    everything = to_heads(keys, values, queries, grad_out)
    kv0, qg0 = everything[:, 0], everything[:, 1]
    kv1_high, qg1_low = shift(everything[per - far :, 0], 1), shift(everything[:far, 1], -1)
    kv1_low, qg1_high = shift(everything[: per - far, 0], 1), shift(everything[far:, 1], -1)
    kv2, qg2 = shift(kv1_high, 1), shift(qg1_low, -1)
    kv1 = [(kv1_low, 0, per - far), (kv1_high, 0, far)]
    qg1 = [(qg1_low, 0, far), (qg1_high, 0, per - far)]

    order = jnp.arange(KB)
    earlier = order[:, None] > order[None, :]
    repeated = jnp.any((listed[:, :, None] == listed[:, None, :]) & earlier, axis=2)
    tiles = listed[:per] - (first_block - (far + per))
    starts = jnp.where(repeated[:per], -(1 << 30), listed[:per] * BLOCK)
    local = listed - first_block
    real = first_block + jnp.arange(listed.shape[0]) < total
    wanted = (local >= 0) & (local < per) & jnp.logical_not(repeated) & real[:, None]
    rank = jnp.sum(jnp.where(wanted[:, None, :] & earlier, 1, 0), axis=2)
    taken = wanted[:, :, None] & (rank[:, :, None] == jnp.arange(KB + GROUP))
    own_tiles = jnp.sum(jnp.where(taken, local[:, :, None], 0), axis=1)
    counts = jnp.sum(wanted.astype(jnp.int32), axis=1)
    base = (first_block * BLOCK).reshape(1)

    late, late_stat = attend(
        tiles, starts, doc_lengths, qg0, half, half, far, [*kv1, (kv0, 0, per)], [], [qg1_low, qg1_high]
    )
    both, stat = attend(
        tiles, starts, doc_lengths, qg0, 0, half, 0,
        [(kv2, 0, far), *kv1, (kv0, 0, half)], [late, late_stat], [qg2],
    )
    attended, grad_q = to_tokens(both)
    grads = key_grads(
        counts, own_tiles, doc_lengths, base, kv0,
        [(qg0, 0, per), *qg1, (qg2, 0, far)],
        [(stat, 0, per), (shift(stat, -1), 0, per), (shift(stat, -2), 0, far)],
    )
    grad_k, grad_v = to_tokens(grads)
    return attended, grad_q, grad_k, grad_v


def solution(mesh):
    blk, head = mesh.devices.shape
    grid = Mesh(mesh.devices.reshape(blk // 2, 2, head), ("yz", "core", "head"))
    rows = P(("yz", "core", "head"), None)
    return jax.shard_map(
        on_device,
        mesh=grid,
        in_specs=(rows, rows, rows, rows, P(("yz", "core"), None), P()),
        out_specs=(rows,) * 4,
        check_vma=False,
    )
```

```python
import functools
import math

import jax
import jax.numpy as jnp
from jax import lax
from jax.experimental import pallas as pl
from jax.experimental.pallas import tpu as pltpu
from jax.sharding import Mesh
from jax.sharding import PartitionSpec as P

HD = 128
BLOCK = 128
KB = 16
WIN = 24
SCALE = HD**-0.5
EXPONENT = SCALE * math.log2(math.e)
GROUP = 4
CORES = ("core", "head")
NN = (((1,), (0,)), ((), ()))
NT = (((1,), (1,)), ((), ()))
TN = (((0,), (0,)), ((), ()))
SMEM = pl.BlockSpec(memory_space=pltpu.SMEM)
VMEM = pl.BlockSpec(memory_space=pltpu.VMEM)
ANYWHERE = pl.BlockSpec(memory_space=pltpu.HBM)


def dot(a, b, dims):
    return lax.dot_general(a, b, dims, preferred_element_type=jnp.float32)


def fold(x, op):
    return op(x.reshape(BLOCK // 8, 8, BLOCK), axis=0)


def rows_of(ref, tiles):
    return jnp.concatenate([ref[tile] for tile in tiles], axis=0)


def part(x, i):
    return x[i * BLOCK : (i + 1) * BLOCK]


def corners(pair):
    zero = jnp.zeros((BLOCK, HD), pair.dtype)
    top = jnp.concatenate([pair[:, :HD], zero], axis=1)
    return jnp.concatenate([top, jnp.concatenate([zero, pair[:, HD:]], axis=1)], axis=0)


def start_copies(pieces, target, sems, first):
    copies, at = [], 0
    for i, (ref, begin, count) in enumerate(pieces):
        copies.append(
            pltpu.make_async_copy(
                ref.at[pl.ds(begin, count)], target.at[pl.ds(at, count)], sems.at[first + i]
            )
        )
        at += count
    for copy in copies:
        copy.start()
    return copies


def doc_starts(doc_ref):
    starts, total = [], jnp.int32(0)
    for d in range(doc_ref.shape[0]):
        starts.append(total)
        total = total + doc_ref[d]
    return starts


def doc_begin(starts, query_pos):
    begin = jnp.zeros_like(query_pos)
    for start in starts:
        begin = jnp.where(start <= query_pos, start, begin)
    return begin


def blocks(count, kind):
    return jax.ShapeDtypeStruct((count, BLOCK, 2 * HD), kind)


def cost(tiles, matmuls):
    return pl.CostEstimate(
        flops=matmuls * tiles * BLOCK * BLOCK * HD // 4,
        bytes_accessed=1 << 20,
        transcendentals=0,
    )


def total_of(pieces):
    return sum(count for _, _, count in pieces)


def queries_kernel(unroll, first, count, shift_by, spans, done,
                   tile_ref, start_ref, doc_ref, qg_ref, *refs):
    kv_refs, refs = refs[: len(spans)], refs[len(spans) :]
    out_ref, stat_ref, kv, s_buf, d_buf, sems = refs[-6:]
    pieces = [(ref, *span) for ref, span in zip(kv_refs, spans)]
    copies = start_copies(pieces, kv, sems, 0)
    if done:
        rest = pl.ds(count, done)
        finished = [
            pltpu.make_async_copy(refs[0], out_ref.at[rest], sems.at[len(spans)]),
            pltpu.make_async_copy(refs[1], stat_ref.at[rest], sems.at[len(spans) + 1]),
        ]
        for copy in finished:
            copy.start()
    starts = doc_starts(doc_ref)
    sub = lax.broadcasted_iota(jnp.int32, (BLOCK, BLOCK), 0)
    lane = lax.broadcasted_iota(jnp.int32, (BLOCK, BLOCK), 1)
    lane_row = lax.broadcasted_iota(jnp.int32, (1, BLOCK), 1)
    for copy in copies:
        copy.wait()

    def one(t, slot):
        s_ref, d_ref = s_buf.at[slot], d_buf.at[slot]
        row = first + t
        qt, gt = qg_ref[row][:, :HD].T, qg_ref[row][:, HD:].T
        tiles = [tile_ref[row, i] - shift_by for i in range(KB)]
        begin = doc_begin(starts, start_ref[row, 0] + lane_row)
        peak = jnp.full((8, BLOCK), -3e38, jnp.float32)
        for j in range(0, KB, GROUP):
            scores = dot(rows_of(kv, tiles[j : j + GROUP])[:, :HD], qt, NN)
            for i in range(j, j + GROUP):
                allowed = sub >= begin - start_ref[row, i]
                if i == 0:
                    allowed = allowed & (sub <= lane)
                s = jnp.where(allowed, part(scores, i - j), -1e30)
                s_ref[i] = s
                peak = jnp.maximum(peak, fold(s, jnp.max))
        for j in range(0, KB, GROUP):
            d_rows = dot(rows_of(kv, tiles[j : j + GROUP])[:, HD:], gt, NN)
            d_ref[pl.ds(j, GROUP)] = d_rows.reshape(GROUP, BLOCK, BLOCK)
        peak = jnp.max(peak, axis=0, keepdims=True) * EXPONENT
        sum_p = jnp.zeros((8, BLOCK), jnp.float32)
        sum_d = jnp.zeros((8, BLOCK), jnp.float32)
        for i in range(KB):
            p = jnp.exp2(s_ref[i] * EXPONENT - peak)
            s_ref[i] = p
            sum_p = sum_p + fold(p, jnp.sum)
            sum_d = sum_d + fold(p * d_ref[i], jnp.sum)
        total = jnp.sum(sum_p, axis=0, keepdims=True)
        inv = 1.0 / total
        delta = jnp.sum(sum_d, axis=0, keepdims=True) * inv
        stat_ref[t, 0:1] = peak + jnp.log2(total)
        stat_ref[t, 1:2] = delta
        attended = jnp.zeros((BLOCK, HD), jnp.float32)
        grad_q = jnp.zeros((BLOCK, HD), jnp.float32)
        for j in range(0, KB, GROUP):
            group = range(j, j + GROUP)
            p = [s_ref[i] * inv for i in group]
            p_low = jnp.concatenate([x.astype(jnp.bfloat16) for x in p], axis=0)
            ds = jnp.concatenate(
                [(p[i - j] * (d_ref[i] - delta)).astype(jnp.bfloat16) for i in group], axis=0
            )
            kv_rows = rows_of(kv, tiles[j : j + GROUP])
            attended += dot(p_low, kv_rows[:, HD:], TN)
            grad_q += dot(ds, kv_rows[:, :HD], TN)
        out_ref[t, :, :HD] = attended.astype(jnp.bfloat16)
        out_ref[t, :, HD:] = (grad_q * SCALE).astype(jnp.bfloat16)

    def step(t, _):
        for u in range(unroll):
            one(t * unroll + u, u)
        return 0

    lax.fori_loop(0, count // unroll, step, 0)
    if done:
        for copy in finished:
            copy.wait()


def attend(tiles, starts, docs, qg, first, count, shift_by, pieces, done, after, unroll=4):
    spans = [piece[1:] for piece in pieces]
    done_rows = done[0].shape[0] if done else 0
    extra = [piece[0] for piece in pieces] + list(done) + list(after)
    return pl.pallas_call(
        functools.partial(queries_kernel, unroll, first, count, shift_by, spans, done_rows),
        out_shape=(
            blocks(count + done_rows, jnp.bfloat16),
            jax.ShapeDtypeStruct((count + done_rows, 2, BLOCK), jnp.float32),
        ),
        in_specs=[SMEM, SMEM, SMEM, VMEM] + [ANYWHERE] * len(extra),
        out_specs=(VMEM, VMEM),
        scratch_shapes=[
            pltpu.VMEM((total_of(pieces), BLOCK, 2 * HD), jnp.bfloat16),
            pltpu.VMEM((unroll, KB, BLOCK, BLOCK), jnp.float32),
            pltpu.VMEM((unroll, KB, BLOCK, BLOCK), jnp.float32),
            pltpu.SemaphoreType.DMA((len(pieces) + 2,)),
        ],
        compiler_params=pltpu.CompilerParams(vmem_limit_bytes=32 << 20),
        cost_estimate=cost(count * KB, 4),
        name="attend",
    )(tiles, starts, docs, qg, *extra)


def keys_kernel(
    unroll, rows, spans, n_qg,
    count_ref, tile_ref, doc_ref, base_ref, kv_ref, *refs,
):
    pieces = [(ref, *span) for ref, span in zip(refs, spans)]
    out_ref, qg, stat, acc, row_of, slot_of, sems = refs[-7:]
    copies = start_copies(pieces[:n_qg], qg, sems, 0)
    copies += start_copies(pieces[n_qg:], stat, sems, n_qg)
    acc[...] = jnp.zeros_like(acc)
    starts = doc_starts(doc_ref)
    base = base_ref[0]
    sub = lax.broadcasted_iota(jnp.int32, (BLOCK, BLOCK), 0)
    lane_row = lax.broadcasted_iota(jnp.int32, (1, BLOCK), 1)

    def list_row(r, at):
        def put(k, at):
            row_of[at] = r
            slot_of[at] = k * GROUP
            return at + 1

        groups = (count_ref[r] + (GROUP - 1)) >> (GROUP.bit_length() - 1)
        return lax.fori_loop(0, groups, put, at)

    items = lax.fori_loop(0, rows, list_row, jnp.int32(0))
    for u in range(unroll):
        row_of[items + u] = 0
        slot_of[items + u] = KB
    for copy in copies:
        copy.wait()

    def one(item):
        r, slot = row_of[item], slot_of[item]
        count = count_ref[r]
        both = corners(qg[r])
        query_pos = base + r * BLOCK + lane_row
        begin = doc_begin(starts, query_pos)
        peak, delta = stat[r, 0:1], stat[r, 1:2]
        tiles = [tile_ref[r, slot + i] for i in range(GROUP)]
        scores = dot(rows_of(kv_ref, tiles), both, NT)
        weights = []
        for i in range(GROUP):
            start = jnp.where(slot + i < count, base + tiles[i] * BLOCK, 1 << 30)
            allowed = (sub >= begin - start) & (sub <= query_pos - start)
            s = part(scores, i)
            p = jnp.where(allowed, jnp.exp2(s[:, :BLOCK] * EXPONENT - peak), 0.0)
            ds = (p * (s[:, BLOCK:] - delta)).astype(jnp.bfloat16)
            weights.append(jnp.concatenate([ds, p.astype(jnp.bfloat16)], axis=1))
        return tiles, dot(jnp.concatenate(weights, axis=0), both, NN)

    def step(t, _):
        results = [one(t * unroll + u) for u in range(unroll)]
        for tiles, grads in results:
            for i in range(GROUP):
                acc[tiles[i]] += part(grads, i)
        return 0

    lax.fori_loop(0, lax.div(items + (unroll - 1), jnp.int32(unroll)), step, 0)
    out_ref[:, :, :HD] = (acc[:, :, :HD] * SCALE).astype(jnp.bfloat16)
    out_ref[:, :, HD:] = acc[:, :, HD:].astype(jnp.bfloat16)


def key_grads(counts, tiles, docs, base, kv, qg, stat, unroll=12):
    per, rows = kv.shape[0], total_of(qg)
    pieces = [*qg, *stat]
    spans = [piece[1:] for piece in pieces]
    items = rows * (KB // GROUP) + unroll
    return pl.pallas_call(
        functools.partial(keys_kernel, unroll, rows, spans, len(qg)),
        out_shape=blocks(per, jnp.bfloat16),
        in_specs=[SMEM, SMEM, SMEM, SMEM, VMEM] + [ANYWHERE] * len(pieces),
        out_specs=VMEM,
        scratch_shapes=[
            pltpu.VMEM((rows, BLOCK, 2 * HD), jnp.bfloat16),
            pltpu.VMEM((rows, 2, BLOCK), jnp.float32),
            pltpu.VMEM((per, BLOCK, 2 * HD), jnp.float32),
            pltpu.SMEM((items,), jnp.int32),
            pltpu.SMEM((items,), jnp.int32),
            pltpu.SemaphoreType.DMA((len(pieces),)),
        ],
        compiler_params=pltpu.CompilerParams(vmem_limit_bytes=32 << 20),
        cost_estimate=cost(rows * 8, 4),
        name="key_grads",
    )(counts, tiles, docs, base, kv, *[piece[0] for piece in pieces])


def run_copies(pairs, sems):
    copies = [
        pltpu.make_async_copy(source, target, sems.at[i])
        for i, (source, target) in enumerate(pairs)
    ]
    for copy in copies:
        copy.start()
    for copy in copies:
        copy.wait()


def columns(i):
    return pl.ds(i * HD, HD)


def pack_kernel(count, *refs):
    ins, (out_ref, held, in_sems, sems) = refs[:count], refs[-4:]
    arrive = [
        pltpu.make_async_copy(ref, held.at[j], in_sems.at[j]) for j, ref in enumerate(ins)
    ]
    for copy in arrive:
        copy.start()
    leave = []
    for j in range(count):
        arrive[j].wait()
        for h in range(out_ref.shape[0]):
            leave.append(
                pltpu.make_async_copy(
                    held.at[j, :, columns(h)],
                    out_ref.at[h, j // 2, :, columns(j % 2)],
                    sems.at[j, h],
                )
            )
            leave[-1].start()
    for copy in leave:
        copy.wait()


def to_heads(*arrays):
    heads = arrays[0].shape[1] // HD
    packed = pl.pallas_call(
        functools.partial(pack_kernel, len(arrays)),
        out_shape=jax.ShapeDtypeStruct((heads, len(arrays) // 2, BLOCK, 2 * HD), jnp.bfloat16),
        in_specs=[ANYWHERE] * len(arrays),
        out_specs=ANYWHERE,
        scratch_shapes=[
            pltpu.VMEM((len(arrays), *arrays[0].shape), jnp.bfloat16),
            pltpu.SemaphoreType.DMA((len(arrays),)),
            pltpu.SemaphoreType.DMA((len(arrays), heads)),
        ],
        name="pack",
    )(*arrays)
    return lax.all_to_all(packed, CORES, 0, 0, tiled=True)


def unpack_kernel(pair_ref, a_ref, b_ref, sems):
    pairs = []
    for h in range(pair_ref.shape[0]):
        for j, ref in enumerate((a_ref, b_ref)):
            pairs.append((pair_ref.at[h, :, columns(j)], ref.at[:, columns(h)]))
    run_copies(pairs, sems)


def to_tokens(pair):
    pair = lax.all_to_all(pair, CORES, 0, 0, tiled=True)
    rows = jax.ShapeDtypeStruct((BLOCK, pair.shape[0] * HD), jnp.bfloat16)
    return pl.pallas_call(
        unpack_kernel,
        out_shape=(rows, rows),
        in_specs=[VMEM],
        out_specs=(ANYWHERE, ANYWHERE),
        scratch_shapes=[pltpu.SemaphoreType.DMA((2 * pair.shape[0],))],
        compiler_params=pltpu.CompilerParams(vmem_limit_bytes=8 << 20),
        name="unpack",
    )(pair)


def shift(value, steps):
    count = lax.axis_size("yz")
    first, last = max(0, -steps), min(count, count - steps)
    return lax.ppermute(value, "yz", [(source, source + steps) for source in range(first, last)])


def on_device(queries, keys, values, grad_out, key_blocks, doc_lengths):
    per = lax.axis_size("core") * lax.axis_size("head")
    total = lax.axis_size("yz") * per
    far, half = WIN - 1 - per, per // 2
    first_block = lax.axis_index("yz") * per

    partner = lax.ppermute(key_blocks, "core", [(0, 1), (1, 0)])
    is_first = lax.axis_index("core") == 0
    listed = jnp.concatenate(
        [jnp.where(is_first, key_blocks, partner), jnp.where(is_first, partner, key_blocks)]
    )
    listed = jnp.concatenate([listed, shift(listed, -1), shift(listed[:far], -2)])
    everything = to_heads(keys, values, queries, grad_out)
    kv0, qg0 = everything[:, 0], everything[:, 1]
    kv1_high, qg1_low = shift(everything[per - far :, 0], 1), shift(everything[:far, 1], -1)
    kv1_low, qg1_high = shift(everything[: per - far, 0], 1), shift(everything[far:, 1], -1)
    kv2, qg2 = shift(kv1_high, 1), shift(qg1_low, -1)
    kv1 = [(kv1_low, 0, per - far), (kv1_high, 0, far)]
    qg1 = [(qg1_low, 0, far), (qg1_high, 0, per - far)]

    order = jnp.arange(KB)
    earlier = order[:, None] > order[None, :]
    repeated = jnp.any((listed[:, :, None] == listed[:, None, :]) & earlier, axis=2)
    tiles = listed[:per] - (first_block - (far + per))
    starts = jnp.where(repeated[:per], -(1 << 30), listed[:per] * BLOCK)
    local = listed - first_block
    real = first_block + jnp.arange(listed.shape[0]) < total
    wanted = (local >= 0) & (local < per) & jnp.logical_not(repeated) & real[:, None]
    rank = jnp.sum(jnp.where(wanted[:, None, :] & earlier, 1, 0), axis=2)
    taken = wanted[:, :, None] & (rank[:, :, None] == jnp.arange(KB + GROUP))
    own_tiles = jnp.sum(jnp.where(taken, local[:, :, None], 0), axis=1)
    counts = jnp.sum(wanted.astype(jnp.int32), axis=1)
    base = (first_block * BLOCK).reshape(1)

    late, late_stat = attend(
        tiles, starts, doc_lengths, qg0, half, half, far, [*kv1, (kv0, 0, per)], [], [qg1_low, qg1_high]
    )
    both, stat = attend(
        tiles, starts, doc_lengths, qg0, 0, half, 0,
        [(kv2, 0, far), *kv1, (kv0, 0, half)], [late, late_stat], [qg2],
    )
    attended, grad_q = to_tokens(both)
    grads = key_grads(
        counts, own_tiles, doc_lengths, base, kv0,
        [(qg0, 0, per), *qg1, (qg2, 0, far)],
        [(stat, 0, per), (shift(stat, -1), 0, per), (shift(stat, -2), 0, far)],
    )
    grad_k, grad_v = to_tokens(grads)
    return attended, grad_q, grad_k, grad_v


def solution(mesh):
    blk, head = mesh.devices.shape
    grid = Mesh(mesh.devices.reshape(blk // 2, 2, head), ("yz", "core", "head"))
    rows = P(("yz", "core", "head"), None)
    return jax.shard_map(
        on_device,
        mesh=grid,
        in_specs=(rows, rows, rows, rows, P(("yz", "core"), None), P()),
        out_specs=(rows,) * 4,
        check_vma=False,
    )
```
